32 devices in a mesh: section: 4 (over y, core), gx: 8 (over z, x).
Axes of the slice: x: 2, y: 2, z: 4, core: 2. Of those that a mesh axis runs over, the one named last changes fastest.
Arguments:
- samples: bfloat16 [2, 1024, 32, 4096], P(None, 'gx', 'section'), may hold values from -8 to 8
- positions: float32 [2, 1024], replicated, may hold values from 0 to 8
- beam_dir: int32 [64], replicated, may hold values from 0 to 63, each once
- load_exp: int32 [4096], P(('section', 'gx')), may hold values from 0 to 3
Outputs:
- beams_out: bfloat16 [2, 64, 32, 4096], P(None, 'gx', 'section')
The draws below stay inside these ranges and needn't reach their ends.
Inputs may be any that keep to these rules, and one draw needn't show every extreme that they name: `beam_dir`: every direction index 0 to 63 belongs to exactly one beam.
All inputs are finite; a program needn't handle non-finite values.
Results may differ from the reference program's by a relative error of at most 0.018.
Values may be sent and summed in bfloat16 or wider, within the bound.
A program may use at most 320 MiB of HBM per device.

```python
import math
import jax
import jax.numpy as jnp
from jax import lax

M = 1024
RADIX = 64
F = 4096
B = 64
TAPS = 4
ITERS = 2
K = 32


def draw_samples(key, part):
    gain_key = jax.random.fold_in(key, 11)
    noise_key = jax.random.fold_in(key, 12)
    gains = jnp.exp(jax.random.uniform(gain_key, (1, M, 1, 1), jnp.float32, math.log(0.3), math.log(3.0)))
    values = gains * jax.random.normal(noise_key, (2, M, K, F), jnp.float32)
    return jnp.clip(values, -8.0, 8.0).astype(jnp.bfloat16)


def with_ends(values, rng, least, largest):
    spot = [jax.random.randint(jax.random.fold_in(rng, axis), (), 0, length) for axis, length in enumerate(values.shape)]
    widest = values.shape.index(max(values.shape))
    neighbour = spot[:widest] + [(spot[widest] + 1) % values.shape[widest]] + spot[widest + 1:]
    return values.at[tuple(spot)].set(least).at[tuple(neighbour)].set(largest)


def setup_inputs(seed: int = 0) -> dict:
    key_of = jax.random.split(jax.random.key(seed), 5)
    samples = draw_samples(jax.random.fold_in(key_of[4], 71), 0)
    positions = jnp.clip(jax.random.uniform(key_of[1], (2, M), jnp.float32, 0.0, 8.0), 0.0, 8.0)
    beam_dir = jax.random.permutation(key_of[2], B).astype(jnp.int32)
    load_exp = with_ends(jax.random.randint(key_of[3], (F,), 0, 4), jax.random.fold_in(key_of[3], 1), 0, 3).astype(jnp.int32)
    return {"samples": samples, "positions": positions, "beam_dir": beam_dir, "load_exp": load_exp}


def prototype(taps_count, length):
    total_len = taps_count * length
    position = jnp.arange(total_len, dtype=jnp.int32).astype(jnp.float32) + 0.5
    window = 0.5 - 0.5 * jnp.cos(2.0 * math.pi / total_len * position)
    shaped = jnp.sinc((position - 0.5 * total_len) / length) * window
    return shaped.reshape(taps_count, length)

def dft_tables(radix_size):
    length = radix_size * radix_size
    counter = jnp.arange(radix_size, dtype=jnp.int32)
    products = counter[:, None] * counter[None, :]
    angles = 2.0 * math.pi / radix_size * (products % radix_size).astype(jnp.float32)
    twiddle = 2.0 * math.pi / length * products.astype(jnp.float32)
    return (jnp.cos(angles).astype(jnp.bfloat16), jnp.sin(angles).astype(jnp.bfloat16), jnp.cos(twiddle), jnp.sin(twiddle))

def contract(matrix, values, pattern):
    return jnp.einsum(pattern, matrix.astype(jnp.float32), values.astype(jnp.float32), precision=lax.Precision.HIGHEST)

def transform(real_part, imag_part, direction_sign, radix_size):
    cosine, sine_table, twist_cos, twist_sin = dft_tables(radix_size)
    leading = real_part.shape[:-1]
    first_real = real_part.reshape(leading + (radix_size, radix_size))
    first_imag = imag_part.reshape(leading + (radix_size, radix_size))
    pattern_one = 'fa,...ab->...fb'
    mid_real = contract(cosine, first_real, pattern_one) - direction_sign * contract(sine_table, first_imag, pattern_one)
    mid_imag = contract(cosine, first_imag, pattern_one) + direction_sign * contract(sine_table, first_real, pattern_one)
    turned_real = (mid_real * twist_cos - direction_sign * mid_imag * twist_sin).astype(jnp.bfloat16)
    turned_imag = (mid_imag * twist_cos + direction_sign * mid_real * twist_sin).astype(jnp.bfloat16)
    pattern_two = 'gb,...fb->...gf'
    out_real = contract(cosine, turned_real, pattern_two) - direction_sign * contract(sine_table, turned_imag, pattern_two)
    out_imag = contract(cosine, turned_imag, pattern_two) + direction_sign * contract(sine_table, turned_real, pattern_two)
    inverse = 1.0 / radix_size
    full_shape = leading + (radix_size * radix_size,)
    return ((out_real * inverse).astype(jnp.bfloat16).reshape(full_shape), (out_imag * inverse).astype(jnp.bfloat16).reshape(full_shape))

def product(pattern, left, right):
    return jnp.einsum(pattern, left.astype(jnp.float32), right.astype(jnp.float32), precision=lax.Precision.HIGHEST)

def beamform(spectra_block, loading, angular, projection):
    x_real = spectra_block[:, 0]
    x_imag = spectra_block[:, 1]
    snapshots = x_real.shape[1]
    phases = angular[:, None, None] * projection[None]
    steer_real = jnp.cos(phases)
    steer_imag = -jnp.sin(phases)
    sol_real = jnp.zeros_like(steer_real)
    sol_imag = jnp.zeros_like(steer_imag)
    res_real, res_imag = (steer_real, steer_imag)
    dir_real, dir_imag = (steer_real, steer_imag)
    residual_power = lax.optimization_barrier(jnp.sum(res_real * res_real + res_imag * res_imag, axis=-1))
    load_col = loading[:, None]
    for sweep_index in range(ITERS):
        low_real = dir_real.astype(jnp.bfloat16)
        low_imag = dir_imag.astype(jnp.bfloat16)
        proj_real = (product('jbm,jkm->jbk', low_real, x_real) + product('jbm,jkm->jbk', low_imag, x_imag)).astype(jnp.bfloat16)
        proj_imag = (product('jbm,jkm->jbk', low_imag, x_real) - product('jbm,jkm->jbk', low_real, x_imag)).astype(jnp.bfloat16)
        image_real = (product('jbk,jkm->jbm', proj_real, x_real) - product('jbk,jkm->jbm', proj_imag, x_imag)) / snapshots + load_col[..., None] * low_real.astype(jnp.float32)
        image_imag = (product('jbk,jkm->jbm', proj_real, x_imag) + product('jbk,jkm->jbm', proj_imag, x_real)) / snapshots + load_col[..., None] * low_imag.astype(jnp.float32)
        proj_wide_real = proj_real.astype(jnp.float32)
        proj_wide_imag = proj_imag.astype(jnp.float32)
        low_wide_real = low_real.astype(jnp.float32)
        low_wide_imag = low_imag.astype(jnp.float32)
        curvature = lax.optimization_barrier(jnp.sum(proj_wide_real * proj_wide_real + proj_wide_imag * proj_wide_imag, axis=-1)) / snapshots + load_col * lax.optimization_barrier(jnp.sum(low_wide_real * low_wide_real + low_wide_imag * low_wide_imag, axis=-1))
        step_size = (residual_power / curvature)[..., None]
        sol_real = sol_real + step_size * dir_real
        sol_imag = sol_imag + step_size * dir_imag
        res_real = res_real - step_size * image_real
        res_imag = res_imag - step_size * image_imag
        new_power = lax.optimization_barrier(jnp.sum(res_real * res_real + res_imag * res_imag, axis=-1))
        ratio = (new_power / residual_power)[..., None]
        dir_real = res_real + ratio * dir_real
        dir_imag = res_imag + ratio * dir_imag
        residual_power = new_power
    mean_sq = lax.optimization_barrier(jnp.mean(sol_real * sol_real + sol_imag * sol_imag, axis=-1)) + 1e-06
    normalizer = lax.rsqrt(sol_real.shape[-1] * mean_sq)[..., None]
    weight_real = (sol_real * normalizer).astype(jnp.bfloat16)
    weight_imag = (sol_imag * normalizer).astype(jnp.bfloat16)
    output_real = (product('jbm,jkm->jbk', weight_real, x_real) + product('jbm,jkm->jbk', weight_imag, x_imag)).astype(jnp.bfloat16)
    output_imag = (product('jbm,jkm->jbk', weight_real, x_imag) - product('jbm,jkm->jbk', weight_imag, x_real)).astype(jnp.bfloat16)
    return jnp.stack([output_real, output_imag], axis=1)

def reference(samples, positions, beam_dir, load_exp):
    shaping = prototype(TAPS, F)
    history = TAPS - 1
    input_block = 16

    def channelize(block_index):
        segment = lax.dynamic_slice_in_dim(samples, block_index * input_block, input_block, 1).astype(jnp.float32)
        padded = jnp.pad(segment, ((0, 0), (0, 0), (history, 0), (0, 0)))
        filtered = shaping[0] * padded[:, :, history:history + K, :]
        for tap_index in range(1, TAPS):
            filtered = filtered + shaping[tap_index] * padded[:, :, history - tap_index:history - tap_index + K, :]
        filtered = filtered.astype(jnp.bfloat16)
        spec_real, spec_imag = transform(filtered[0], filtered[1], -1.0, RADIX)
        return jnp.stack([spec_real, spec_imag])
    blocks = lax.map(channelize, jnp.arange(M // input_block, dtype=jnp.int32))
    spectra = jnp.transpose(blocks, (4, 1, 3, 0, 2)).reshape(F, 2, K, M)
    angle_beam = math.pi / B * (beam_dir.astype(jnp.float32) + 0.5) - 0.5 * math.pi
    projection = jnp.sin(angle_beam)[:, None] * positions[0][None, :] + jnp.cos(angle_beam)[:, None] * positions[1][None, :]
    loading = jnp.exp2(load_exp.astype(jnp.float32))
    freq_all = 2.0 * math.pi * (0.75 + 0.5 * jnp.arange(F, dtype=jnp.int32).astype(jnp.float32) / F)
    channel_block = 16
    block_count = F // channel_block
    outputs = lax.map(lambda members: beamform(members[0], members[1], members[2], projection), (spectra.reshape(block_count, channel_block, 2, K, M), loading.reshape(block_count, channel_block), freq_all.reshape(block_count, channel_block)))
    beam_spec = outputs.reshape(F, 2, B, K)
    ordered = jnp.transpose(beam_spec, (1, 2, 3, 0))
    time_real, time_imag = transform(ordered[0], ordered[1], 1.0, RADIX)
    series = jnp.stack([time_real, time_imag]).astype(jnp.float32)
    padded = jnp.pad(series, ((0, 0), (0, 0), (history, 0), (0, 0)))
    summed = shaping[TAPS - 1] * padded[:, :, history:history + K, :]
    for tap_index in range(1, TAPS):
        summed = summed + shaping[TAPS - 1 - tap_index] * padded[:, :, history - tap_index:history - tap_index + K, :]
    return summed.astype(jnp.bfloat16)
```

```python
import math

import jax
import jax.numpy as jnp
from jax import lax
from jax.sharding import PartitionSpec as P

RADIX = 64
TAPS = 4
ITERS = 2
PIECES = 4


def from_behind(value, axis, steps):
    count = lax.axis_size(axis)
    initial, last = (max(0, -steps), min(count, count - steps))
    return lax.ppermute(value, axis, [(source, source + steps) for source in range(initial, last)])


def for_sending(x):
    return jax.tree.map(lambda a: a.astype(jnp.bfloat16) if a.dtype == jnp.float32 else a, x)


def prototype(taps_count, length):
    total_len = taps_count * length
    position = jnp.arange(total_len, dtype=jnp.int32).astype(jnp.float32) + 0.5
    window = 0.5 - 0.5 * jnp.cos(2.0 * math.pi / total_len * position)
    shaped = jnp.sinc((position - 0.5 * total_len) / length) * window
    return shaped.reshape(taps_count, length)


def dft_tables(radix_size):
    length = radix_size * radix_size
    counter = jnp.arange(radix_size, dtype=jnp.int32)
    products = counter[:, None] * counter[None, :]
    angles = 2.0 * math.pi / radix_size * (products % radix_size).astype(jnp.float32)
    twiddle = 2.0 * math.pi / length * products.astype(jnp.float32)
    return (
        jnp.cos(angles).astype(jnp.bfloat16),
        jnp.sin(angles).astype(jnp.bfloat16),
        jnp.cos(twiddle),
        jnp.sin(twiddle),
    )


def stacked_tables(direction_sign):
    cosine, sine_table, twist_cos, twist_sin = dft_tables(RADIX)
    signed = (direction_sign * sine_table.astype(jnp.float32)).astype(jnp.bfloat16)
    top = jnp.concatenate([cosine, -signed], axis=1)
    bottom = jnp.concatenate([signed, cosine], axis=1)
    return jnp.concatenate([top, bottom], axis=0), twist_cos, direction_sign * twist_sin


def halo_filter(samples):
    block_dev = samples.shape[2]
    history = TAPS - 1
    shaping = prototype(TAPS, samples.shape[3])
    earlier = from_behind(samples[:, :, block_dev - history :, :], "section", 1)
    extended = jnp.concatenate([earlier, samples], axis=2)
    filtered = shaping[0] * extended[:, :, history : history + block_dev, :].astype(jnp.float32)
    for tap_index in range(1, TAPS):
        filtered = filtered + shaping[tap_index] * extended[
            :, :, history - tap_index : history - tap_index + block_dev, :
        ].astype(jnp.float32)
    return filtered.astype(jnp.bfloat16)


def first_stage(filtered):
    _, inputs_dev, block_dev, _ = filtered.shape
    matrix, twist_cos, twist_sin = stacked_tables(-1.0)
    by_input = jnp.transpose(
        filtered.reshape(2, inputs_dev, block_dev, RADIX, RADIX), (2, 0, 3, 4, 1)
    ).reshape(block_dev, 2 * RADIX, RADIX * inputs_dev)
    mid = jnp.einsum("fi,kiz->kfz", matrix, by_input, preferred_element_type=jnp.float32)
    mid = mid.reshape(block_dev, 2, RADIX, RADIX, inputs_dev)
    cos_col, sin_col = twist_cos[..., None], twist_sin[..., None]
    real = (mid[:, 0] * cos_col - mid[:, 1] * sin_col).astype(jnp.bfloat16)
    imag = (mid[:, 1] * cos_col + mid[:, 0] * sin_col).astype(jnp.bfloat16)
    return jnp.concatenate([real, imag], axis=2)


def second_stage(turned):
    matrix, _, _ = stacked_tables(-1.0)
    out = jnp.einsum("gl,kalm->kagm", matrix, turned, preferred_element_type=jnp.float32)
    return (out * (1.0 / RADIX)).astype(jnp.bfloat16)


def rotation(scale, delay):
    phase = scale[:, None, None] * delay[None]
    return jnp.cos(phase), -jnp.sin(phase)


def local_products(spectra, steer):
    chans, _, snapshots, _ = spectra.shape
    x_real, x_imag = spectra[:, 0], spectra[:, 1]
    upper = jnp.concatenate([x_real, x_imag], axis=-1)
    lower = jnp.concatenate([-x_imag, x_real], axis=-1)
    blocked = jnp.concatenate([upper, lower], axis=1)
    projected = jnp.einsum("fbm,fkm->fbk", steer, blocked, preferred_element_type=jnp.float32)
    gram = jnp.einsum("fqm,fkm->fqk", upper, blocked, preferred_element_type=jnp.float32)
    row = jnp.arange(snapshots)[:, None]
    col = jnp.arange(snapshots)[None, :]
    packed = jnp.where(row <= col, gram[..., :snapshots], gram[..., snapshots:])
    return projected.astype(jnp.bfloat16), packed


def solve(projected, packed, loading, inputs_all):
    snapshots = packed.shape[-1]
    row = jnp.arange(snapshots)[:, None]
    col = jnp.arange(snapshots)[None, :]
    flipped = jnp.swapaxes(packed, 1, 2)
    gram_real = jnp.where(row <= col, packed, flipped)
    gram_imag = jnp.where(row < col, -flipped, jnp.where(row > col, packed, 0.0))
    gram = jnp.concatenate(
        [
            jnp.concatenate([gram_real, gram_imag], axis=2),
            jnp.concatenate([-gram_imag, gram_real], axis=2),
        ],
        axis=1,
    )
    y = projected.astype(jnp.float32)
    v = jnp.einsum("fbq,fqk->fbk", y, gram, precision=lax.Precision.HIGHEST)
    load = loading[:, None]
    n1 = jnp.sum(y * y, axis=-1)
    n2 = jnp.sum(y * v, axis=-1)
    spread = n2 - n1 * n1 / inputs_all
    curv_first = n1 / snapshots + load * inputs_all
    alpha_first = inputs_all / curv_first
    h = alpha_first / snapshots
    power = h * h * spread
    beta = power / inputs_all
    along = h * n1 / inputs_all + beta
    second = along[..., None] * y - h[..., None] * v
    curv_second = jnp.sum(second * second, axis=-1) / snapshots + load * (
        power + beta * beta * inputs_all
    )
    alpha_second = power / curv_second
    on_steer = alpha_first + alpha_second * along
    on_image = -alpha_second * h
    lean = on_steer + on_image * n1 / inputs_all
    mean_sq = (lean * lean * inputs_all + on_image * on_image * spread) / inputs_all + 1e-06
    normalizer = lax.rsqrt(inputs_all * mean_sq)
    formed = (normalizer * on_steer)[..., None] * y + (normalizer * on_image)[..., None] * v
    return jnp.stack(
        [formed[..., :snapshots], -formed[..., snapshots:]], axis=0
    ).astype(jnp.bfloat16)


def synthesis_transform(values):
    matrix, twist_cos, twist_sin = stacked_tables(1.0)
    _, beams, blocks, _, _ = values.shape
    rows = beams * blocks
    z = jnp.transpose(values.reshape(2, rows, RADIX, RADIX), (0, 3, 1, 2)).reshape(
        2 * RADIX, rows * RADIX
    )
    mid = jnp.einsum("fi,iz->fz", matrix, z, preferred_element_type=jnp.float32)
    mid = mid.reshape(2, RADIX, rows, RADIX)
    cos_col, sin_col = twist_cos[:, None, :], twist_sin[:, None, :]
    real = (mid[0] * cos_col - mid[1] * sin_col).astype(jnp.bfloat16)
    imag = (mid[1] * cos_col + mid[0] * sin_col).astype(jnp.bfloat16)
    turned = jnp.concatenate([real, imag], axis=2)
    out = jnp.einsum("gl,arl->rga", matrix, turned, preferred_element_type=jnp.float32)
    out = (out * (1.0 / RADIX)).astype(jnp.bfloat16).reshape(
        beams, blocks, 2, RADIX * RADIX
    )
    return jnp.transpose(out, (2, 0, 1, 3))


def body(samples, positions, beam_dir, load_exp):
    section_count = lax.axis_size("section")
    group_count = lax.axis_size("gx")
    section = lax.axis_index("section")
    group = lax.axis_index("gx")
    inputs_dev = samples.shape[1]
    inputs_all = positions.shape[1]
    block_dev = samples.shape[2]
    snapshots = block_dev * section_count
    length = samples.shape[3]
    history = TAPS - 1
    shaping = prototype(TAPS, length)
    beam_total = beam_dir.shape[0]
    beam_dev = beam_total // group_count
    rows_dev = RADIX // section_count
    rows_piece = rows_dev // PIECES
    chans_own = rows_piece * RADIX // group_count

    loading = jnp.exp2(load_exp.astype(jnp.float32))
    loading = lax.all_gather(loading, ("section", "gx"), tiled=True)
    loading = jnp.transpose(loading.reshape(RADIX, RADIX))
    loading = lax.dynamic_slice_in_dim(loading, section * rows_dev, rows_dev, 0)
    loading = loading.reshape(PIECES, group_count, chans_own)
    loading = lax.dynamic_index_in_dim(loading, group, 1, keepdims=False)

    angle_beam = math.pi / beam_total * (beam_dir.astype(jnp.float32) + 0.5) - 0.5 * math.pi
    mine = lax.dynamic_slice_in_dim(positions, group * inputs_dev, inputs_dev, 1)
    delay = (
        jnp.sin(angle_beam)[:, None] * mine[0][None, :]
        + jnp.cos(angle_beam)[:, None] * mine[1][None, :]
    )
    rows = (section * rows_dev + jnp.arange(rows_dev, dtype=jnp.int32)).astype(jnp.float32)
    low_cos, low_sin = rotation(2.0 * math.pi * (0.75 + 0.5 * rows / length), delay)
    steps = jnp.arange(RADIX, dtype=jnp.int32).astype(jnp.float32)
    high_cos, high_sin = rotation(math.pi * RADIX / length * steps, delay)

    turned = first_stage(halo_filter(samples))
    turned = turned.reshape(
        block_dev, section_count, rows_dev, 2 * RADIX, inputs_dev
    )
    formed = []
    for piece in range(PIECES):
        span = slice(piece * rows_piece, (piece + 1) * rows_piece)
        part = turned[:, :, span].reshape(
            block_dev, section_count * rows_piece, 2 * RADIX, inputs_dev
        )
        spectra = second_stage(part).reshape(
            block_dev, section_count, rows_piece, 2, RADIX, inputs_dev
        )
        spectra = jnp.transpose(spectra, (1, 0, 2, 3, 4, 5))
        spectra = lax.all_to_all(spectra, "section", split_axis=0, concat_axis=0, tiled=True)
        spectra = spectra.reshape(snapshots, rows_piece, 2, RADIX, inputs_dev)
        spectra = jnp.transpose(spectra, (1, 3, 2, 0, 4)).reshape(
            rows_piece * RADIX, 2, snapshots, inputs_dev
        )
        lc, ls = low_cos[span][:, None], low_sin[span][:, None]
        steer = jnp.concatenate(
            [lc * high_cos - ls * high_sin, lc * high_sin + ls * high_cos], axis=-1
        ).astype(jnp.bfloat16)
        steer = steer.reshape(rows_piece * RADIX, beam_total, 2 * inputs_dev)
        projected, packed = local_products(spectra, steer)
        projected = lax.psum_scatter(projected, "gx", scatter_dimension=0, tiled=True)
        packed = lax.psum_scatter(packed, "gx", scatter_dimension=0, tiled=True)
        formed.append(solve(projected, packed, loading[piece], inputs_all))

    beam_spec = jnp.stack(formed, axis=1)
    shaped = beam_spec.reshape(
        2, PIECES, chans_own, group_count, beam_dev, section_count, block_dev
    )
    packed_back = jnp.transpose(shaped, (0, 3, 4, 5, 6, 1, 2)).reshape(
        2, group_count, beam_dev, section_count, block_dev * PIECES * chans_own
    )
    returned = lax.all_to_all(
        lax.all_to_all(packed_back, "gx", split_axis=1, concat_axis=1, tiled=True),
        "section",
        split_axis=3,
        concat_axis=3,
        tiled=True,
    )
    opened = returned.reshape(
        2, group_count, beam_dev, section_count, block_dev, PIECES, chans_own
    )
    by_beam = jnp.transpose(opened, (0, 2, 4, 3, 5, 1, 6)).reshape(
        2, beam_dev, block_dev, RADIX, RADIX
    )
    series = synthesis_transform(by_beam).astype(jnp.float32)
    margin_zeros = jnp.zeros((2, beam_dev, history, length), jnp.float32)
    padded = jnp.concatenate([margin_zeros, series, margin_zeros], axis=2)
    out_span = block_dev + history
    summed = shaping[TAPS - 1] * padded[:, :, history : history + out_span, :]
    for tap_index in range(1, TAPS):
        summed = (
            summed
            + shaping[TAPS - 1 - tap_index]
            * padded[:, :, history - tap_index : history - tap_index + out_span, :]
        )
    incoming = from_behind(for_sending(summed[:, :, block_dev:, :]), "section", 1)
    local_part = summed[:, :, :block_dev, :]
    carried = jnp.concatenate(
        [incoming, jnp.zeros((2, beam_dev, block_dev - history, length), jnp.float32)], axis=2
    )
    return (local_part + carried).astype(jnp.bfloat16)


def solution(mesh):
    placed = (P(None, "gx", "section", None), P(), P(), P(("section", "gx")))
    return jax.shard_map(
        body, mesh=mesh, in_specs=placed, out_specs=P(None, "gx", "section", None), check_vma=False
    )
```

```python
import math

import jax
import jax.numpy as jnp
from jax import lax
from jax.sharding import PartitionSpec as P

RADIX = 64
TAPS = 4
ITERS = 2
PIECES = 4


def from_behind(value, axis, steps):
    count = lax.axis_size(axis)
    initial, last = (max(0, -steps), min(count, count - steps))
    return lax.ppermute(value, axis, [(source, source + steps) for source in range(initial, last)])


def for_sending(x):
    return jax.tree.map(lambda a: a.astype(jnp.bfloat16) if a.dtype == jnp.float32 else a, x)


def prototype(taps_count, length):
    total_len = taps_count * length
    position = jnp.arange(total_len, dtype=jnp.int32).astype(jnp.float32) + 0.5
    window = 0.5 - 0.5 * jnp.cos(2.0 * math.pi / total_len * position)
    shaped = jnp.sinc((position - 0.5 * total_len) / length) * window
    return shaped.reshape(taps_count, length)


def dft_tables(radix_size):
    length = radix_size * radix_size
    counter = jnp.arange(radix_size, dtype=jnp.int32)
    products = counter[:, None] * counter[None, :]
    angles = 2.0 * math.pi / radix_size * (products % radix_size).astype(jnp.float32)
    twiddle = 2.0 * math.pi / length * products.astype(jnp.float32)
    return (
        jnp.cos(angles).astype(jnp.bfloat16),
        jnp.sin(angles).astype(jnp.bfloat16),
        jnp.cos(twiddle),
        jnp.sin(twiddle),
    )


def stacked_tables(direction_sign):
    cosine, sine_table, twist_cos, twist_sin = dft_tables(RADIX)
    signed = (direction_sign * sine_table.astype(jnp.float32)).astype(jnp.bfloat16)
    top = jnp.concatenate([cosine, -signed], axis=1)
    bottom = jnp.concatenate([signed, cosine], axis=1)
    return jnp.concatenate([top, bottom], axis=0), twist_cos, direction_sign * twist_sin


def halo_filter(samples):
    block_dev = samples.shape[2]
    history = TAPS - 1
    shaping = prototype(TAPS, samples.shape[3])
    earlier = from_behind(samples[:, :, block_dev - history :, :], "section", 1)
    extended = jnp.concatenate([earlier, samples], axis=2)
    filtered = shaping[0] * extended[:, :, history : history + block_dev, :].astype(jnp.float32)
    for tap_index in range(1, TAPS):
        filtered = filtered + shaping[tap_index] * extended[
            :, :, history - tap_index : history - tap_index + block_dev, :
        ].astype(jnp.float32)
    return filtered.astype(jnp.bfloat16)


def first_stage(filtered):
    _, inputs_dev, block_dev, _ = filtered.shape
    matrix, twist_cos, twist_sin = stacked_tables(-1.0)
    by_input = jnp.transpose(
        filtered.reshape(2, inputs_dev, block_dev, RADIX, RADIX), (2, 0, 3, 4, 1)
    ).reshape(block_dev, 2 * RADIX, RADIX * inputs_dev)
    mid = jnp.einsum("fi,kiz->kfz", matrix, by_input, preferred_element_type=jnp.float32)
    mid = mid.reshape(block_dev, 2, RADIX, RADIX, inputs_dev)
    cos_col, sin_col = twist_cos[..., None], twist_sin[..., None]
    real = (mid[:, 0] * cos_col - mid[:, 1] * sin_col).astype(jnp.bfloat16)
    imag = (mid[:, 1] * cos_col + mid[:, 0] * sin_col).astype(jnp.bfloat16)
    return jnp.concatenate([real, imag], axis=2)


def second_stage(turned):
    matrix, _, _ = stacked_tables(-1.0)
    out = jnp.einsum("gl,kalm->kagm", matrix, turned, preferred_element_type=jnp.float32)
    return (out * (1.0 / RADIX)).astype(jnp.bfloat16)


def rotation(scale, delay):
    phase = scale[:, None, None] * delay[None]
    return jnp.cos(phase), -jnp.sin(phase)


def local_products(spectra, steer):
    chans, _, snapshots, _ = spectra.shape
    x_real, x_imag = spectra[:, 0], spectra[:, 1]
    upper = jnp.concatenate([x_real, x_imag], axis=-1)
    lower = jnp.concatenate([-x_imag, x_real], axis=-1)
    blocked = jnp.concatenate([upper, lower], axis=1)
    projected = jnp.einsum("fbm,fkm->fbk", steer, blocked, preferred_element_type=jnp.float32)
    gram = jnp.einsum("fqm,fkm->fqk", upper, blocked, preferred_element_type=jnp.float32)
    row = jnp.arange(snapshots)[:, None]
    col = jnp.arange(snapshots)[None, :]
    packed = jnp.where(row <= col, gram[..., :snapshots], gram[..., snapshots:])
    return projected.astype(jnp.bfloat16), packed


def solve(projected, packed, loading, inputs_all):
    snapshots = packed.shape[-1]
    row = jnp.arange(snapshots)[:, None]
    col = jnp.arange(snapshots)[None, :]
    flipped = jnp.swapaxes(packed, 1, 2)
    gram_real = jnp.where(row <= col, packed, flipped)
    gram_imag = jnp.where(row < col, -flipped, jnp.where(row > col, packed, 0.0))
    gram = jnp.concatenate(
        [
            jnp.concatenate([gram_real, gram_imag], axis=2),
            jnp.concatenate([-gram_imag, gram_real], axis=2),
        ],
        axis=1,
    )
    y = projected.astype(jnp.float32)
    v = jnp.einsum("fbq,fqk->fbk", y, gram, precision=lax.Precision.HIGHEST)
    load = loading[:, None]
    n1 = jnp.sum(y * y, axis=-1)
    n2 = jnp.sum(y * v, axis=-1)
    spread = n2 - n1 * n1 / inputs_all
    curv_first = n1 / snapshots + load * inputs_all
    alpha_first = inputs_all / curv_first
    h = alpha_first / snapshots
    power = h * h * spread
    beta = power / inputs_all
    along = h * n1 / inputs_all + beta
    second = along[..., None] * y - h[..., None] * v
    curv_second = jnp.sum(second * second, axis=-1) / snapshots + load * (
        power + beta * beta * inputs_all
    )
    alpha_second = power / curv_second
    on_steer = alpha_first + alpha_second * along
    on_image = -alpha_second * h
    lean = on_steer + on_image * n1 / inputs_all
    mean_sq = (lean * lean * inputs_all + on_image * on_image * spread) / inputs_all + 1e-06
    normalizer = lax.rsqrt(inputs_all * mean_sq)
    formed = (normalizer * on_steer)[..., None] * y + (normalizer * on_image)[..., None] * v
    return jnp.stack(
        [formed[..., :snapshots], -formed[..., snapshots:]], axis=0
    ).astype(jnp.bfloat16)


def synthesis_transform(values):
    matrix, twist_cos, twist_sin = stacked_tables(1.0)
    _, beams, blocks, _, _ = values.shape
    rows = beams * blocks
    z = jnp.transpose(values.reshape(2, rows, RADIX, RADIX), (0, 3, 1, 2)).reshape(
        2 * RADIX, rows * RADIX
    )
    mid = jnp.einsum("fi,iz->fz", matrix, z, preferred_element_type=jnp.float32)
    mid = mid.reshape(2, RADIX, rows, RADIX)
    cos_col, sin_col = twist_cos[:, None, :], twist_sin[:, None, :]
    real = (mid[0] * cos_col - mid[1] * sin_col).astype(jnp.bfloat16)
    imag = (mid[1] * cos_col + mid[0] * sin_col).astype(jnp.bfloat16)
    turned = jnp.concatenate([real, imag], axis=2)
    out = jnp.einsum("gl,arl->rga", matrix, turned, preferred_element_type=jnp.float32)
    out = (out * (1.0 / RADIX)).astype(jnp.bfloat16).reshape(
        beams, blocks, 2, RADIX * RADIX
    )
    return jnp.transpose(out, (2, 0, 1, 3))


def body(samples, positions, beam_dir, load_exp):
    section_count = lax.axis_size("section")
    group_count = lax.axis_size("gx")
    section = lax.axis_index("section")
    group = lax.axis_index("gx")
    inputs_dev = samples.shape[1]
    inputs_all = positions.shape[1]
    block_dev = samples.shape[2]
    snapshots = block_dev * section_count
    length = samples.shape[3]
    history = TAPS - 1
    shaping = prototype(TAPS, length)
    beam_total = beam_dir.shape[0]
    beam_dev = beam_total // group_count
    rows_dev = RADIX // section_count
    rows_piece = rows_dev // PIECES
    chans_own = rows_piece * RADIX // group_count

    loading = jnp.exp2(load_exp.astype(jnp.float32))
    loading = lax.all_gather(loading, ("section", "gx"), tiled=True)
    loading = jnp.transpose(loading.reshape(RADIX, RADIX))
    loading = lax.dynamic_slice_in_dim(loading, section * rows_dev, rows_dev, 0)
    loading = loading.reshape(PIECES, group_count, chans_own)
    loading = lax.dynamic_index_in_dim(loading, group, 1, keepdims=False)

    angle_beam = math.pi / beam_total * (beam_dir.astype(jnp.float32) + 0.5) - 0.5 * math.pi
    mine = lax.dynamic_slice_in_dim(positions, group * inputs_dev, inputs_dev, 1)
    delay = (
        jnp.sin(angle_beam)[:, None] * mine[0][None, :]
        + jnp.cos(angle_beam)[:, None] * mine[1][None, :]
    )
    rows = (section * rows_dev + jnp.arange(rows_dev, dtype=jnp.int32)).astype(jnp.float32)
    low_cos, low_sin = rotation(2.0 * math.pi * (0.75 + 0.5 * rows / length), delay)
    steps = jnp.arange(RADIX, dtype=jnp.int32).astype(jnp.float32)
    high_cos, high_sin = rotation(math.pi * RADIX / length * steps, delay)

    samples, loading = lax.optimization_barrier((samples, loading))
    turned = first_stage(halo_filter(samples))
    turned = turned.reshape(
        block_dev, section_count, rows_dev, 2 * RADIX, inputs_dev
    )
    formed = []
    for piece in range(PIECES):
        span = slice(piece * rows_piece, (piece + 1) * rows_piece)
        part = turned[:, :, span].reshape(
            block_dev, section_count * rows_piece, 2 * RADIX, inputs_dev
        )
        spectra = second_stage(part).reshape(
            block_dev, section_count, rows_piece, 2, RADIX, inputs_dev
        )
        spectra = jnp.transpose(spectra, (1, 0, 2, 3, 4, 5))
        spectra = lax.all_to_all(spectra, "section", split_axis=0, concat_axis=0, tiled=True)
        spectra = spectra.reshape(snapshots, rows_piece, 2, RADIX, inputs_dev)
        spectra = jnp.transpose(spectra, (1, 3, 2, 0, 4)).reshape(
            rows_piece * RADIX, 2, snapshots, inputs_dev
        )
        lc, ls = low_cos[span][:, None], low_sin[span][:, None]
        steer = jnp.concatenate(
            [lc * high_cos - ls * high_sin, lc * high_sin + ls * high_cos], axis=-1
        ).astype(jnp.bfloat16)
        steer = steer.reshape(rows_piece * RADIX, beam_total, 2 * inputs_dev)
        projected, packed = local_products(spectra, steer)
        chans = projected.shape[0]
        projected = lax.psum_scatter(
            projected.reshape(chans, -1), "gx", scatter_dimension=0, tiled=True
        ).reshape(-1, beam_total, 2 * snapshots)
        packed = lax.psum_scatter(
            packed.reshape(chans, -1), "gx", scatter_dimension=0, tiled=True
        ).reshape(-1, snapshots, snapshots)
        formed.append(solve(projected, packed, loading[piece], inputs_all))

    beam_spec = jnp.stack(formed, axis=1)
    shaped = beam_spec.reshape(
        2, PIECES, chans_own, group_count, beam_dev, section_count, block_dev
    )
    packed_back = jnp.transpose(shaped, (0, 3, 4, 5, 6, 1, 2)).reshape(
        2, group_count, beam_dev, section_count, block_dev * PIECES * chans_own
    )
    returned = lax.all_to_all(
        lax.all_to_all(packed_back, "gx", split_axis=1, concat_axis=1, tiled=True),
        "section",
        split_axis=3,
        concat_axis=3,
        tiled=True,
    )
    opened = returned.reshape(
        2, group_count, beam_dev, section_count, block_dev, PIECES, chans_own
    )
    by_beam = jnp.transpose(opened, (0, 2, 4, 3, 5, 1, 6)).reshape(
        2, beam_dev, block_dev, RADIX, RADIX
    )
    series = synthesis_transform(by_beam).astype(jnp.float32)
    margin_zeros = jnp.zeros((2, beam_dev, history, length), jnp.float32)
    padded = jnp.concatenate([margin_zeros, series, margin_zeros], axis=2)
    out_span = block_dev + history
    summed = shaping[TAPS - 1] * padded[:, :, history : history + out_span, :]
    for tap_index in range(1, TAPS):
        summed = (
            summed
            + shaping[TAPS - 1 - tap_index]
            * padded[:, :, history - tap_index : history - tap_index + out_span, :]
        )
    incoming = from_behind(for_sending(summed[:, :, block_dev:, :]), "section", 1)
    local_part = summed[:, :, :block_dev, :]
    carried = jnp.concatenate(
        [incoming, jnp.zeros((2, beam_dev, block_dev - history, length), jnp.float32)], axis=2
    )
    return (local_part + carried).astype(jnp.bfloat16)


def solution(mesh):
    placed = (P(None, "gx", "section", None), P(), P(), P(("section", "gx")))
    return jax.shard_map(
        body, mesh=mesh, in_specs=placed, out_specs=P(None, "gx", "section", None), check_vma=False
    )
```

```python
import math

import jax
import jax.numpy as jnp
from jax import lax
from jax.experimental import pallas as pl
from jax.experimental.pallas import tpu as pltpu
from jax.sharding import PartitionSpec as P

RADIX = 64
TAPS = 4
ITERS = 2
PIECES = 2


def from_behind(value, axis, steps):
    count = lax.axis_size(axis)
    initial, last = (max(0, -steps), min(count, count - steps))
    return lax.ppermute(value, axis, [(source, source + steps) for source in range(initial, last)])


def for_sending(x):
    return jax.tree.map(lambda a: a.astype(jnp.bfloat16) if a.dtype == jnp.float32 else a, x)


def prototype(taps_count, length):
    total_len = taps_count * length
    position = jnp.arange(total_len, dtype=jnp.int32).astype(jnp.float32) + 0.5
    window = 0.5 - 0.5 * jnp.cos(2.0 * math.pi / total_len * position)
    shaped = jnp.sinc((position - 0.5 * total_len) / length) * window
    return shaped.reshape(taps_count, length)


def dft_tables(radix_size):
    length = radix_size * radix_size
    counter = jnp.arange(radix_size, dtype=jnp.int32)
    products = counter[:, None] * counter[None, :]
    angles = 2.0 * math.pi / radix_size * (products % radix_size).astype(jnp.float32)
    twiddle = 2.0 * math.pi / length * products.astype(jnp.float32)
    return (
        jnp.cos(angles).astype(jnp.bfloat16),
        jnp.sin(angles).astype(jnp.bfloat16),
        jnp.cos(twiddle),
        jnp.sin(twiddle),
    )


def stacked_tables(direction_sign):
    cosine, sine_table, twist_cos, twist_sin = dft_tables(RADIX)
    signed = (direction_sign * sine_table.astype(jnp.float32)).astype(jnp.bfloat16)
    top = jnp.concatenate([cosine, -signed], axis=1)
    bottom = jnp.concatenate([signed, cosine], axis=1)
    return jnp.concatenate([top, bottom], axis=0), twist_cos, direction_sign * twist_sin


def with_halo(samples):
    block_dev = samples.shape[2]
    turned = jnp.transpose(samples, (2, 0, 3, 1))
    earlier = from_behind(turned[block_dev - (TAPS - 1) :], "section", 1)
    return jnp.concatenate([earlier, turned], axis=0)


def split_rows(matrix, parts):
    rows = matrix.reshape(2, parts, RADIX // parts, matrix.shape[1])
    return jnp.transpose(rows, (1, 0, 2, 3)).reshape(matrix.shape)


def analysis_kernel(parts, x3, x2, x1, x0, proto, first, second, tcos, tsin, *rest):
    outs, (filt, turn) = rest[:-2], rest[-2:]
    length = x0.shape[2]
    chunk = 128

    def filter_step(step, carry):
        rows = pl.ds(pl.multiple_of(step * chunk, chunk), chunk)
        for c in range(2):
            total = proto[0, rows, :] * x0[0, c, rows, :].astype(jnp.float32)
            for tap, ref in ((1, x1), (2, x2), (3, x3)):
                total = total + proto[tap, rows, :] * ref[0, c, rows, :].astype(jnp.float32)
            place = pl.ds(pl.multiple_of(c * length + step * chunk, chunk), chunk)
            filt[place, :] = total
        return carry

    lax.fori_loop(0, length // chunk, filter_step, 0)

    def first_step(l, carry):
        z = jnp.concatenate(
            [filt[pl.ds(l, RADIX, stride=RADIX), :], filt[pl.ds(length + l, RADIX, stride=RADIX), :]],
            axis=0,
        ).astype(jnp.bfloat16)
        mid = jnp.dot(first[...], z, preferred_element_type=jnp.float32)
        real, imag = mid[:RADIX], mid[RADIX:]
        cos_col, sin_col = tcos[l], tsin[l]
        turn[pl.ds(l, RADIX, stride=RADIX), :] = real * cos_col - imag * sin_col
        turn[pl.ds(length + l, RADIX, stride=RADIX), :] = imag * cos_col + real * sin_col
        return carry

    lax.fori_loop(0, RADIX, first_step, 0, unroll=8)

    rows_piece = RADIX // len(outs)
    wide = 2 * RADIX // parts
    for piece, out in enumerate(outs):

        def second_step(a, carry, piece=piece, out=out):
            base = pl.multiple_of((piece * rows_piece + a) * RADIX, RADIX)
            t = jnp.concatenate(
                [turn[pl.ds(base, RADIX), :], turn[pl.ds(base + length, RADIX), :]], axis=0
            ).astype(jnp.bfloat16)
            spec = jnp.dot(second[...], t, preferred_element_type=jnp.float32)
            spec = (spec * (1.0 / RADIX)).astype(jnp.bfloat16)
            for part in range(parts):
                out[part, 0, a] = spec[part * wide : (part + 1) * wide]
            return carry

        lax.fori_loop(0, rows_piece, second_step, 0, unroll=8)


def analysis(samples, parts):
    extended = with_halo(samples)
    blocks = extended.shape[0] - (TAPS - 1)
    _, _, length, inputs_dev = extended.shape
    matrix, twist_cos, twist_sin = stacked_tables(-1.0)
    second = split_rows(matrix, parts)
    shaping = prototype(TAPS, length)
    rows_piece = RADIX // PIECES
    wide = 2 * RADIX // parts
    if inputs_dev % 128 == 0:
        proto = jnp.broadcast_to(shaping[..., None], (TAPS, length, inputs_dev))
        table = (RADIX, RADIX, inputs_dev)
        tcos = jnp.broadcast_to(jnp.transpose(twist_cos)[..., None], table)
        tsin = jnp.broadcast_to(jnp.transpose(twist_sin)[..., None], table)

        def whole(shape):
            return pl.BlockSpec(shape, lambda k: (0,) * len(shape), pipeline_mode=pl.Buffered(1))

        def shifted(shift):
            return pl.BlockSpec((1, 2, length, inputs_dev), lambda k: (k + shift, 0, 0, 0))

        return pl.pallas_call(
            lambda *refs: analysis_kernel(parts, *refs),
            grid=(blocks,),
            in_specs=[shifted(p) for p in range(TAPS)]
            + [whole(v.shape) for v in (proto, matrix, second, tcos, tsin)],
            out_specs=[
                pl.BlockSpec((parts, 1, rows_piece, wide, inputs_dev), lambda k: (0, k, 0, 0, 0))
            ]
            * PIECES,
            out_shape=[
                jax.ShapeDtypeStruct((parts, blocks, rows_piece, wide, inputs_dev), jnp.bfloat16)
            ]
            * PIECES,
            scratch_shapes=[pltpu.VMEM((2 * length, inputs_dev), jnp.float32)] * 2,
            compiler_params=pltpu.CompilerParams(vmem_limit_bytes=56 * 1024 * 1024),
            cost_estimate=pl.CostEstimate(
                flops=blocks * inputs_dev * length * 1024,
                bytes_accessed=blocks * inputs_dev * length * 20,
                transcendentals=0,
            ),
        )(extended, extended, extended, extended, proto, matrix, second, tcos, tsin)
    filtered = sum(
        shaping[p][:, None] * extended[TAPS - 1 - p : TAPS - 1 - p + blocks].astype(jnp.float32)
        for p in range(TAPS)
    ).astype(jnp.bfloat16)
    z = filtered.reshape(blocks, 2 * RADIX, RADIX * inputs_dev)
    mid = jnp.einsum("fi,kiz->kfz", matrix, z, preferred_element_type=jnp.float32)
    mid = mid.reshape(blocks, 2, RADIX, RADIX, inputs_dev)
    cos_col, sin_col = twist_cos[..., None], twist_sin[..., None]
    real = (mid[:, 0] * cos_col - mid[:, 1] * sin_col).astype(jnp.bfloat16)
    imag = (mid[:, 1] * cos_col + mid[:, 0] * sin_col).astype(jnp.bfloat16)
    turned = jnp.concatenate([real, imag], axis=2)
    out = jnp.einsum("gl,kalm->kagm", second, turned, preferred_element_type=jnp.float32)
    out = (out * (1.0 / RADIX)).astype(jnp.bfloat16)
    out = out.reshape(blocks, PIECES, rows_piece, parts, wide, inputs_dev)
    out = jnp.transpose(out, (1, 3, 0, 2, 4, 5))
    return [out[piece] for piece in range(PIECES)]


def rotation(scale, delay):
    phase = scale[:, None, None] * delay[None]
    return jnp.cos(phase), -jnp.sin(phase)


def local_products(spectra, steer):
    chans, _, snapshots, _ = spectra.shape
    x_real, x_imag = spectra[:, 0], spectra[:, 1]
    upper = jnp.concatenate([x_real, x_imag], axis=-1)
    lower = jnp.concatenate([-x_imag, x_real], axis=-1)
    blocked = jnp.concatenate([upper, lower], axis=1)
    projected = jnp.einsum("fbm,fkm->fbk", steer, blocked, preferred_element_type=jnp.float32)
    gram = jnp.einsum("fqm,fkm->fqk", upper, blocked, preferred_element_type=jnp.float32)
    row = jnp.arange(snapshots)[:, None]
    col = jnp.arange(snapshots)[None, :]
    packed = jnp.where(row <= col, gram[..., :snapshots], gram[..., snapshots:])
    return projected.astype(jnp.bfloat16), packed


def solve(projected, packed, loading, inputs_all):
    snapshots = packed.shape[-1]
    row = jnp.arange(snapshots)[:, None]
    col = jnp.arange(snapshots)[None, :]
    flipped = jnp.swapaxes(packed, 1, 2)
    gram_real = jnp.where(row <= col, packed, flipped)
    gram_imag = jnp.where(row < col, -flipped, jnp.where(row > col, packed, 0.0))
    gram = jnp.concatenate(
        [
            jnp.concatenate([gram_real, gram_imag], axis=2),
            jnp.concatenate([-gram_imag, gram_real], axis=2),
        ],
        axis=1,
    )
    y = projected.astype(jnp.float32)
    v = jnp.einsum("fbq,fqk->fbk", y, gram, precision=lax.Precision.HIGHEST)
    load = loading[:, None]
    n1 = jnp.sum(y * y, axis=-1)
    n2 = jnp.sum(y * v, axis=-1)
    spread = n2 - n1 * n1 / inputs_all
    curv_first = n1 / snapshots + load * inputs_all
    alpha_first = inputs_all / curv_first
    h = alpha_first / snapshots
    power = h * h * spread
    beta = power / inputs_all
    along = h * n1 / inputs_all + beta
    second = along[..., None] * y - h[..., None] * v
    curv_second = jnp.sum(second * second, axis=-1) / snapshots + load * (
        power + beta * beta * inputs_all
    )
    alpha_second = power / curv_second
    on_steer = alpha_first + alpha_second * along
    on_image = -alpha_second * h
    lean = on_steer + on_image * n1 / inputs_all
    mean_sq = (lean * lean * inputs_all + on_image * on_image * spread) / inputs_all + 1e-06
    normalizer = lax.rsqrt(inputs_all * mean_sq)
    formed = (normalizer * on_steer)[..., None] * y + (normalizer * on_image)[..., None] * v
    return jnp.stack(
        [formed[..., :snapshots], -formed[..., snapshots:]], axis=0
    ).astype(jnp.bfloat16)


def synthesis_transform(values):
    matrix, twist_cos, twist_sin = stacked_tables(1.0)
    _, beams, blocks, pieces, _, rows_piece = values.shape
    rows = beams * blocks
    z = jnp.transpose(
        values.reshape(2, rows, pieces, RADIX, rows_piece), (0, 3, 1, 2, 4)
    ).reshape(2 * RADIX, rows * RADIX)
    mid = jnp.einsum("fi,iz->fz", matrix, z, preferred_element_type=jnp.float32)
    mid = mid.reshape(2, RADIX, rows, RADIX)
    cos_col, sin_col = twist_cos[:, None, :], twist_sin[:, None, :]
    real = (mid[0] * cos_col - mid[1] * sin_col).astype(jnp.bfloat16)
    imag = (mid[1] * cos_col + mid[0] * sin_col).astype(jnp.bfloat16)
    turned = jnp.concatenate([real, imag], axis=2)
    out = jnp.einsum("gl,arl->rga", matrix, turned, preferred_element_type=jnp.float32)
    out = (out * (1.0 / RADIX)).astype(jnp.bfloat16).reshape(
        beams, blocks, 2, RADIX * RADIX
    )
    return jnp.transpose(out, (2, 0, 1, 3))


def body(samples, positions, beam_dir, load_exp):
    section_count = lax.axis_size("section")
    group_count = lax.axis_size("gx")
    section = lax.axis_index("section")
    group = lax.axis_index("gx")
    inputs_dev = samples.shape[1]
    inputs_all = positions.shape[1]
    block_dev = samples.shape[2]
    snapshots = block_dev * section_count
    length = samples.shape[3]
    history = TAPS - 1
    shaping = prototype(TAPS, length)
    beam_total = beam_dir.shape[0]
    beam_dev = beam_total // group_count
    highs_dev = RADIX // section_count
    rows_piece = RADIX // PIECES
    chans_piece = highs_dev * rows_piece
    chans_own = chans_piece // group_count

    loading = jnp.exp2(load_exp.astype(jnp.float32))
    if highs_dev % group_count == 0:
        loading = loading.reshape(-1, PIECES, rows_piece)
    else:
        loading = lax.all_gather(loading, ("section", "gx"), tiled=True)
        loading = loading.reshape(section_count, highs_dev, PIECES, rows_piece)[section]
        loading = jnp.transpose(loading, (1, 0, 2)).reshape(PIECES, group_count, chans_own)
        loading = jnp.transpose(loading[:, group].reshape(PIECES, 1, chans_own), (1, 0, 2))
    loading = jnp.transpose(loading, (1, 0, 2)).reshape(PIECES * chans_own)

    angle_beam = math.pi / beam_total * (beam_dir.astype(jnp.float32) + 0.5) - 0.5 * math.pi
    mine = lax.dynamic_slice_in_dim(positions, group * inputs_dev, inputs_dev, 1)
    delay = (
        jnp.sin(angle_beam)[:, None] * mine[0][None, :]
        + jnp.cos(angle_beam)[:, None] * mine[1][None, :]
    )
    rows = jnp.arange(RADIX, dtype=jnp.int32).astype(jnp.float32)
    low_cos, low_sin = rotation(2.0 * math.pi * (0.75 + 0.5 * rows / length), delay)
    steps = (section * highs_dev + jnp.arange(highs_dev, dtype=jnp.int32)).astype(jnp.float32)
    high_cos, high_sin = rotation(math.pi * RADIX / length * steps, delay)
    high_cos, high_sin = high_cos[:, None], high_sin[:, None]

    projections, grams = [], []
    for piece, spectra in enumerate(analysis(samples, section_count)):
        span = slice(piece * rows_piece, (piece + 1) * rows_piece)
        spectra = lax.all_to_all(spectra, "section", split_axis=0, concat_axis=0, tiled=True)
        spectra = spectra.reshape(snapshots, rows_piece, 2, highs_dev, inputs_dev)
        spectra = jnp.transpose(spectra, (3, 1, 2, 0, 4)).reshape(
            chans_piece, 2, snapshots, inputs_dev
        )
        lc, ls = low_cos[span], low_sin[span]
        steer = jnp.concatenate(
            [lc * high_cos - ls * high_sin, lc * high_sin + ls * high_cos], axis=-1
        ).astype(jnp.bfloat16)
        steer = steer.reshape(chans_piece, beam_total, 2 * inputs_dev)
        projected, packed = local_products(spectra, steer)
        projections.append(
            lax.psum_scatter(
                projected.reshape(chans_piece, -1), "gx", scatter_dimension=0, tiled=True
            )
        )
        grams.append(packed.reshape(group_count, chans_own, -1))
    packed = jnp.concatenate(grams, axis=1).reshape(group_count * PIECES * chans_own, -1)
    packed = lax.psum_scatter(packed, "gx", scatter_dimension=0, tiled=True)
    beam_spec = solve(
        jnp.concatenate(projections, axis=0).reshape(-1, beam_total, 2 * snapshots),
        packed.reshape(-1, snapshots, snapshots),
        loading,
        inputs_all,
    )
    shaped = beam_spec.reshape(
        2, PIECES, chans_own, group_count, beam_dev, section_count, block_dev
    )
    packed_back = jnp.transpose(shaped, (0, 3, 4, 5, 6, 1, 2)).reshape(
        2, group_count, beam_dev, section_count, block_dev * PIECES * chans_own
    )
    returned = lax.all_to_all(
        lax.all_to_all(packed_back, "gx", split_axis=1, concat_axis=1, tiled=True),
        "section",
        split_axis=3,
        concat_axis=3,
        tiled=True,
    )
    opened = returned.reshape(
        2, group_count, beam_dev, section_count, block_dev, PIECES, chans_own
    )
    by_beam = jnp.transpose(opened, (0, 2, 4, 5, 3, 1, 6)).reshape(
        2, beam_dev, block_dev, PIECES, RADIX, rows_piece
    )
    series = synthesis_transform(by_beam).astype(jnp.float32)
    margin_zeros = jnp.zeros((2, beam_dev, history, length), jnp.float32)
    padded = jnp.concatenate([margin_zeros, series, margin_zeros], axis=2)
    out_span = block_dev + history
    summed = shaping[TAPS - 1] * padded[:, :, history : history + out_span, :]
    for tap_index in range(1, TAPS):
        summed = (
            summed
            + shaping[TAPS - 1 - tap_index]
            * padded[:, :, history - tap_index : history - tap_index + out_span, :]
        )
    incoming = from_behind(for_sending(summed[:, :, block_dev:, :]), "section", 1)
    local_part = summed[:, :, :block_dev, :]
    carried = jnp.concatenate(
        [incoming, jnp.zeros((2, beam_dev, block_dev - history, length), jnp.float32)], axis=2
    )
    return (local_part + carried).astype(jnp.bfloat16)


def solution(mesh):
    placed = (P(None, "gx", "section", None), P(), P(), P(("section", "gx")))
    return jax.shard_map(
        body, mesh=mesh, in_specs=placed, out_specs=P(None, "gx", "section", None), check_vma=False
    )
```
